512 devices in a mesh: ctx: 32 (over z, core), head: 8 (over y, x_lo), dp: 2 (over x_hi).
Axes of the slice: x: 4 (x_hi: 2, x_lo: 2; x = x_hi * 2 + x_lo), y: 4, z: 16, core: 2. Of those that a mesh axis runs over, the one named last changes fastest.
Arguments:
- queries: bfloat16 [16384, 4096], P(('dp', 'ctx'), 'head'), parts along dimension 0, may hold values from -12 to 12
- keys_values: bfloat16 [2, 16384, 1024], P(None, ('dp', 'ctx'), 'head'), parts along dimension 1, may hold values from -12 to 12
- positions: int32 [16384], P(('dp', 'ctx')), parts along dimension 0, may hold values from 0 to 4096, as said below
- offsets: int32 [16], P('dp'), parts along dimension 0, may hold values from 0 to 8190, as said below
- w_out: bfloat16 [4096, 4096], P('head'), may hold values from -0.375 to 0.375
Outputs:
- mixed: bfloat16 [16384, 4096], P(('dp', 'ctx'), 'head'), parts along dimension 0
The draws below stay inside these ranges and needn't reach their ends.
There are 2 independent parts, one for each index of `dp`. The reference program is written for one: setup_inputs(seed, part) draws one part's arguments, and reference() takes and returns one part's arrays. A program takes and returns all parts, laid end to end along the dimension named above; an argument that names none is the same for every part. Nothing has to cross between parts.
Inputs may be any that keep to these rules, and one draw needn't show every extreme that they name: offsets[0] = 0 and the offsets rise strictly; the first document holds exactly 4097 tokens and every later one two or more. positions[t] = t minus the largest offset not above t.
All inputs are finite; a program needn't handle non-finite values.
Results may differ from the reference program's by a relative error of at most 0.02.
Values may be sent and summed in bfloat16 or wider, within the bound.
A program may use at most 128 MiB of HBM per device.

```python
import math
import jax
import jax.numpy as jnp
from jax import lax

D = 4096
HD = 128
QH_DEV = 4
NDOC = 8
KV_HEADS = 8
HEADS = 32
SEQ = 8192


def document_starts(key):
    second = SEQ // 2 + 1
    pool = SEQ - SEQ // 2 - NDOC - 1
    picked = jax.random.permutation(jax.random.fold_in(key, 11), pool)[:NDOC - 2]
    picked = jnp.sort(picked) + second + 2 + jnp.arange(NDOC - 2)
    return jnp.concatenate([jnp.zeros((1,), jnp.int32), jnp.full((1,), second, jnp.int32), picked.astype(jnp.int32)])


def draw_offsets(key, part):
    return document_starts(key)


def draw_positions(key, part):
    starts = document_starts(key)
    index = jnp.arange(SEQ, dtype=jnp.int32)
    owner = jnp.max(jnp.where(starts[None, :] <= index[:, None], starts[None, :], 0), axis=1)
    return (index - owner).astype(jnp.int32)


def row_scales(key, lowest, highest):
    return jnp.exp(jax.random.uniform(key, (SEQ, 1), jnp.float32, math.log(lowest), math.log(highest)))


def base_field(key, shape):
    return jnp.clip(jax.random.normal(key, shape, jnp.float32), -4.0, 4.0)


def draw_queries(key, part):
    scales = row_scales(jax.random.fold_in(key, 31), 0.3, 3.0)
    field = base_field(jax.random.fold_in(key, 32), (SEQ, HEADS * HD)) * scales
    return field.astype(jnp.bfloat16)


def draw_keys_values(key, part):
    scales = row_scales(jax.random.fold_in(key, 41), 0.15, 0.55)
    keys = base_field(jax.random.fold_in(key, 42), (SEQ, KV_HEADS * HD)) * scales
    values = base_field(jax.random.fold_in(key, 43), (SEQ, KV_HEADS * HD))
    return jnp.stack([keys, values]).astype(jnp.bfloat16)


def spiked(result, rng, source, target, parts, factor):
    def block_of(axis_at):
        return (jnp.arange(result.shape[axis_at]) // (result.shape[axis_at] // parts)).reshape((-1,) + (1,) * (result.ndim - 1 - axis_at))

    first = jax.random.permutation(rng, parts)[block_of(target)]
    far = (block_of(target) + parts // 2) % parts
    return jnp.where((block_of(source) == first) | (block_of(source) == far), factor * result, result)


def shard_levels(stream_key, extent, cuts, least, top_value):
    gain, own = 1.0, jax.random.fold_in(stream_key, 6)
    for position, parts in cuts:
        steps = jnp.exp(jax.random.uniform(jax.random.fold_in(own, position), (parts,), jnp.float32, least / len(cuts), top_value / len(cuts)))
        gain = gain * jnp.repeat(steps, extent[position] // parts).reshape([-1 if axis == position else 1 for axis in range(len(extent))])
    return gain


def noise_with(stream_key, dims, scale, bound, pieces, heavy, held_as=jnp.bfloat16):
    result = scale * jax.random.normal(stream_key, dims, jnp.float32)
    if pieces:
        result = result * shard_levels(stream_key, dims, pieces, -0.22, 0.18)
    return jnp.clip(spiked(result, jax.random.fold_in(stream_key, 3), *heavy), -bound, bound).astype(held_as)


def setup_inputs(seed: int = 0, part: int = 0) -> dict:
    key_of = jax.random.split(jax.random.key(seed), 6)
    own_keys = jax.random.split(jax.random.fold_in(key_of[5], part), 6)
    return {
        "queries": draw_queries(jax.random.fold_in(jax.random.fold_in(key_of[5], part), 71), part),
        "keys_values": draw_keys_values(jax.random.fold_in(jax.random.fold_in(key_of[5], part), 71), part),
        "positions": draw_positions(jax.random.fold_in(jax.random.fold_in(key_of[5], part), 71), part),
        "offsets": draw_offsets(jax.random.fold_in(jax.random.fold_in(key_of[5], part), 71), part),
        "w_out": noise_with(key_of[4], (HEADS * HD, D), (4 * HD) ** -0.5, 0.375, ((0, 8),), (0, 1, 8, 2.0)),
    }


ROPE_BASE = 500000.0
STRETCH = 16.0
ANCHOR_LENGTH = 8192.0
BETA_FAST = 32.0
BETA_SLOW = 1.0
MAGNITUDE = 0.1 * math.log(16.0) + 1.0
NEGATIVE = -1.0e30


def tables(positions, width):
    half = width // 2
    index = jnp.arange(half, dtype=jnp.float32)
    base_freq = jnp.exp(index * (-2.0 * math.log(ROPE_BASE) / width))
    ratio = base_freq * (ANCHOR_LENGTH / (2.0 * math.pi))
    ramp = jnp.clip((ratio - BETA_SLOW) / (BETA_FAST - BETA_SLOW), 0.0, 1.0)
    freq = base_freq * (1.0 - ramp) / STRETCH + base_freq * ramp
    angle = positions.astype(jnp.float32)[:, None] * freq[None, :]
    return jnp.cos(angle) * MAGNITUDE, jnp.sin(angle) * MAGNITUDE


def rotate(field, cosine, sine):
    half = field.shape[-1] // 2
    first = field[..., :half]
    second = field[..., half:]
    cos_rows = cosine[:, None, :]
    sin_rows = sine[:, None, :]
    return jnp.concatenate([first * cos_rows - second * sin_rows, second * cos_rows + first * sin_rows], axis=-1)


def reference(queries, keys_values, positions, offsets, w_out):
    cosine, sine = tables(positions, HD)
    rot_queries = (rotate(queries.reshape(SEQ, HEADS, HD).astype(jnp.float32), cosine, sine) * (HD ** -0.5)).astype(jnp.bfloat16)
    rot_keys = rotate(keys_values[0].reshape(SEQ, KV_HEADS, HD).astype(jnp.float32), cosine, sine).astype(jnp.bfloat16)
    values = keys_values[1].reshape(SEQ, KV_HEADS, HD)
    index = jnp.arange(SEQ, dtype=jnp.int32)
    starts = jnp.max(jnp.where(offsets[None, :] <= index[:, None], offsets[None, :], 0), axis=1).astype(jnp.int32)
    block = math.gcd(SEQ, 1024)
    count = SEQ // block
    grouped = rot_queries.reshape(count, block, KV_HEADS, QH_DEV, HD).transpose(2, 0, 1, 3, 4)
    key_heads = rot_keys.transpose(1, 0, 2)
    value_heads = values.transpose(1, 0, 2)
    query_index = index.reshape(count, block)
    query_start = starts.reshape(count, block)

    def one_group(group_args):
        group_q, key_rows, value_rows = group_args

        def one_block(block_args):
            block_q, rows_index, rows_start = block_args
            scores = jnp.einsum("qhd,kd->qhk", block_q.astype(jnp.float32), key_rows.astype(jnp.float32))
            visible = (index[None, :] <= rows_index[:, None]) & (index[None, :] >= rows_start[:, None])
            visible = visible[:, None, :]
            peak = jnp.max(jnp.where(visible, scores, NEGATIVE), axis=2, keepdims=True)
            expo = jnp.where(visible, jnp.exp(scores - peak), 0.0)
            total = jnp.sum(expo, axis=2)
            weights = expo.astype(jnp.bfloat16)
            summed = jnp.einsum("qhk,kd->qhd", weights.astype(jnp.float32), value_rows.astype(jnp.float32))
            return (summed / total[..., None]).astype(jnp.bfloat16)

        return lax.map(one_block, (group_q, query_index, query_start))

    attended = lax.map(one_group, (grouped, key_heads, value_heads))
    attended = attended.transpose(1, 2, 0, 3, 4).reshape(SEQ, HEADS * HD)
    width = QH_DEV * HD
    mixed = jnp.zeros((SEQ, D), jnp.float32)
    for group in range(KV_HEADS):
        partial_value = jnp.dot(attended[:, group * width:(group + 1) * width], w_out[group * width:(group + 1) * width], preferred_element_type=jnp.float32).astype(jnp.bfloat16)
        partial_value = lax.optimization_barrier(partial_value)
        mixed = mixed + partial_value.astype(jnp.float32)
    return mixed.astype(jnp.bfloat16)
```

```python
import functools
import math

import jax
import jax.numpy as jnp
from jax import lax
from jax.experimental import pallas as pl
from jax.experimental.pallas import tpu as pltpu
from jax.sharding import PartitionSpec as P

HD = 128
QH = 4
ROPE_BASE = 500000.0
STRETCH = 16.0
ANCHOR_LENGTH = 8192.0
BETA_FAST = 32.0
BETA_SLOW = 1.0
MAGNITUDE = 0.1 * math.log(16.0) + 1.0
NEGATIVE = -1e30
LOG2E = 1.4426950408889634
MESH = pl.DeviceIdType.MESH
BF = jnp.bfloat16
F32 = jnp.float32


def remote(src, dst, send_sem, recv_sem, device):
    return pltpu.make_async_remote_copy(
        src_ref=src, dst_ref=dst, send_sem=send_sem, recv_sem=recv_sem,
        device_id=device, device_id_type=MESH,
    )


def dot(a, b):
    return jnp.dot(a, b, preferred_element_type=F32)


def dot_t(a, b):
    return lax.dot_general(a, b, (((1,), (1,)), ((), ())), preferred_element_type=F32)


def kernel(
    nc, nh, rows,
    q_ref, kv_ref, off_ref, w_ref, out_ref,
    qs, kvb, st, mx, acc, w2, att, attp, ysb, yrb, xq, xp, xr,
    up_s, peer_s, kv_r, wl_s, ws_s, wr_s, wf_s, wf_r, ax_s, ax_r, y_s, y_r, xq_s, xq_r, xr_s, xr_r,
):
    nhalf = nc // 2
    nz = nhalf // 2
    ny = nh // 2
    half_rows = rows // 2
    mrows = 2 * half_rows
    width = QH * HD
    wrows = width // 2

    c = lax.axis_index("ctx")
    hd = lax.axis_index("head")
    dp = lax.axis_index("dp")
    z = c // 2
    core = c % 2
    half = z // nz
    zz = z % nz
    own = 2 * zz + core
    other = 2 * zz + 1 - core
    y = hd // 2
    x = hd % 2
    up = {"ctx": jnp.minimum(c + 2, nc - 1)}
    down = {"ctx": jnp.maximum(c - 2, 0)}
    peer = {"ctx": c + 1 - 2 * core}
    across = {"head": hd + 1 - 2 * x}
    same_dp = x == core
    w_to = {"head": hd + 1 - 2 * x, "dp": jnp.where(same_dp, dp, 1 - dp)}
    w_from = {"head": hd + 1 - 2 * x, "dp": jnp.where(same_dp, 1 - dp, dp)}
    extra = nhalf

    def along_y(j):
        return {"head": ((y + j) % ny) * 2 + x}

    barrier = pltpu.get_barrier_semaphore()

    def greet(device):
        pl.semaphore_signal(barrier, inc=1, device_id=device, device_id_type=MESH)

    greet(peer)
    greet(across)
    greet(w_to)
    greet(w_from)
    for j in range(1, ny):
        greet(along_y(j))

    @pl.when(zz < nz - 1)
    def _():
        greet(up)

    @pl.when(zz > 0)
    def _():
        greet(down)

    @pl.when(c < nhalf)
    def _():
        greet({"ctx": jnp.int32(extra)})

    @pl.when(c == extra)
    def _():
        def body(d, carry):
            greet({"ctx": d})
            return carry
        lax.fori_loop(0, nhalf, body, 0)

    def own_weights(j):
        col = pl.multiple_of((((y + j) % ny) * 2 + x) * width, 128)
        return pltpu.make_async_copy(
            w_ref.at[:, pl.ds(col, width)], w2.at[j, pl.ds(0, width), :], wl_s.at[j])

    for j in range(ny):
        own_weights(j).start()

    lane = lax.broadcasted_iota(jnp.int32, (rows, HD), 1)
    token = lax.broadcasted_iota(jnp.int32, (rows, HD), 0) + c * rows
    start = jnp.zeros((rows, HD), jnp.int32)
    for d in range(off_ref.shape[0]):
        o = off_ref[d]
        start = jnp.maximum(start, jnp.where(token >= o, o, 0))
    st[...] = start
    index = (lax.broadcasted_iota(jnp.int32, (8, HD), 1) % (HD // 2)).astype(F32)
    base = jnp.exp(index * (-2.0 * math.log(ROPE_BASE) / HD))
    ramp = jnp.clip((base * (ANCHOR_LENGTH / (2.0 * math.pi)) - BETA_SLOW) / (BETA_FAST - BETA_SLOW), 0.0, 1.0)
    freq = base * (1.0 - ramp) / STRETCH + base * ramp
    angle = (token - start).astype(F32) * freq[0:1]
    cosine = jnp.cos(angle) * MAGNITUDE
    sine = jnp.sin(angle) * jnp.where(lane < HD // 2, -MAGNITUDE, MAGNITUDE)

    def rotate(field):
        field = field.astype(F32)
        return field * cosine + pltpu.roll(field, HD // 2, 1) * sine

    kvb[own, 1] = kv_ref[1]
    kvb[own, 0] = rotate(kv_ref[0]).astype(BF)

    pl.semaphore_wait(
        barrier,
        4 + (ny - 1)
        + jnp.where(zz < nz - 1, 1, 0) + jnp.where(zz > 0, 1, 0)
        + jnp.where(c < nhalf, 1, 0) + jnp.where(c == extra, nhalf, 0),
    )

    def send_up(slot, i, step):
        return remote(kvb.at[slot, i], kvb.at[slot, i], up_s.at[step, i], kv_r.at[slot, i], up)

    def send_peer(slot, i, step):
        return remote(kvb.at[slot, i], kvb.at[slot, i], peer_s.at[step, i], kv_r.at[slot, i], peer)

    @pl.when(zz < nz - 1)
    def _():
        for i in (1, 0):
            send_up(own, i, 0).start()
    for i in (1, 0):
        send_peer(own, i, 0).start()

    wrow = pl.multiple_of(core * wrows, 128)
    wback = pl.multiple_of((1 - core) * wrows, 128)

    def send_weights(j):
        col = pl.multiple_of((((y + j) % ny) * 2 + 1 - x) * width, 128)
        return remote(
            w_ref.at[pl.ds(wrow, wrows), pl.ds(col, width)],
            w2.at[j, pl.ds(width + wrow, wrows), :], ws_s.at[j], wr_s.at[j], w_to)

    def pass_weights(j):
        at = w2.at[j, pl.ds(width + wrow, wrows), :]
        return remote(at, at, wf_s.at[j], wf_r.at[j], peer)

    def passed_weights(j):
        at = w2.at[j, pl.ds(width + wback, wrows), :]
        return remote(at, at, wf_s.at[j], wf_r.at[j], peer)

    for j in range(ny):
        send_weights(j).start()

    def forward_weights():
        for j in range(ny):
            send_weights(j).wait_recv()
            pass_weights(j).start()

    scale = HD ** (-0.5) * LOG2E
    for h in range(QH):
        rot = (rotate(q_ref[:, h * HD:(h + 1) * HD]) * scale).astype(BF)
        for r in range(2):
            at = (r * QH + h) * half_rows
            qs[at:at + half_rows, :] = rot[r * half_rows:(r + 1) * half_rows]

    def send_xq(d):
        return remote(xq, xq, xq_s.at[d], xq_r, {"ctx": d})

    @pl.when(c == extra)
    def _():
        heads = [qs[h * half_rows:h * half_rows + 1, :] for h in range(QH)]
        xq[...] = jnp.concatenate(heads + [jnp.zeros((16 - QH, HD), BF)], axis=0)

        def body(d, carry):
            send_xq(d).start()
            return carry
        lax.fori_loop(0, nhalf, body, 0)

    def with_ones(v):
        return jnp.concatenate([v, jnp.ones(v.shape, BF)], axis=1)

    def wide(v, n):
        return jnp.tile(v, (1, n))

    def starts_of(t):
        r = t // (QH // 2)
        part = st[r * half_rows:(r + 1) * half_rows, :]
        return jnp.concatenate([part] * 2, axis=0)

    def tokens_of(t, n):
        r = t // (QH // 2)
        i = lax.broadcasted_iota(jnp.int32, (mrows, n), 0) % half_rows
        return i + (c * rows + r * half_rows)

    ntile = QH

    for t in range(ntile):
        at = slice(t * mrows, (t + 1) * mrows)
        s = dot_t(qs[at, :], kvb[own, 0])
        key = lax.broadcasted_iota(jnp.int32, (mrows, rows), 1) + c * rows
        seen = (key <= tokens_of(t, rows)) & (key >= wide(starts_of(t), rows // HD))
        s = jnp.where(seen, s, NEGATIVE)
        m = jnp.broadcast_to(jnp.max(s, axis=1, keepdims=True), (mrows, HD))
        p = jnp.exp2(s - wide(m, rows // HD)).astype(BF)
        mx[at, :] = m
        acc[at, :] = dot(p, with_ones(kvb[own, 1]))

    def update(first, keys, values, masked):
        n = keys.shape[0]
        values = with_ones(values)
        for t in range(ntile):
            at = slice(t * mrows, (t + 1) * mrows)
            s = dot_t(qs[at, :], keys)
            if masked:
                key = lax.broadcasted_iota(jnp.int32, (mrows, n), 1) + first
                s = jnp.where(key >= wide(starts_of(t), n // HD), s, NEGATIVE)
            before = mx[at, :]
            m = jnp.maximum(before, jnp.max(s, axis=1, keepdims=True))
            p = jnp.exp2(s - wide(m, n // HD)).astype(BF)
            alpha = jnp.exp2(before - m)
            mx[at, :] = m
            acc[at, :] = acc[at, :] * wide(alpha, 2) + dot(p, values)

    def send_xp():
        return remote(xp, xr.at[own], xr_s, xr_r.at[own], {"ctx": jnp.int32(extra)})

    @pl.when(c < nhalf)
    def _():
        send_xq(0).wait_recv()
        s = dot_t(xq[...], kvb[own, 0])
        m = jnp.broadcast_to(jnp.max(s, axis=1, keepdims=True), (16, HD))
        p = jnp.exp2(s - wide(m, rows // HD)).astype(BF)
        xp[:, 0:HD] = m[0:8]
        xp[:, HD:] = dot(p, with_ones(kvb[own, 1]))[0:8]
        send_xp().start()

    for i in (1, 0):
        send_peer(other, i, 0).wait_recv()

    @pl.when(core == 1)
    def _():
        update((c - 1) * rows, kvb[other, 0], kvb[other, 1], True)

    late = min(5, nz - 1)

    def step(k, carry):
        chip = zz - k
        mine = 2 * chip + core
        theirs = 2 * chip + 1 - core
        for i in (1, 0):
            send_up(mine, i, 0).wait_recv()

            @pl.when(zz < nz - 1)
            def _():
                send_up(mine, i, k).start()
            send_peer(mine, i, k).start()
        for i in (1, 0):
            send_peer(theirs, i, 0).wait_recv()
        keys = jnp.concatenate([kvb[2 * chip, 0], kvb[2 * chip + 1, 0]], axis=0)
        values = jnp.concatenate([kvb[2 * chip, 1], kvb[2 * chip + 1, 1]], axis=0)

        @pl.when(half == 0)
        def _():
            update(0, keys, values, False)

        @pl.when(half == 1)
        def _():
            update((half * nhalf + 2 * chip) * rows, keys, values, True)

        @pl.when(k == late)
        def _():
            forward_weights()
        return carry

    lax.fori_loop(1, zz + 1, step, 0)

    @pl.when(zz < late)
    def _():
        forward_weights()

    @pl.when(c == extra)
    def _():
        def arrived(d, carry):
            remote(xp, xr.at[d], xr_s, xr_r.at[d], {"ctx": jnp.int32(0)}).wait_recv()
            return carry
        lax.fori_loop(0, nhalf, arrived, 0)
        pad = [jnp.zeros((8 - QH, HD), F32)]
        mo = jnp.concatenate([mx[h * half_rows:h * half_rows + 1, :] for h in range(QH)] + pad, axis=0)
        ao = jnp.concatenate(
            [acc[h * half_rows:h * half_rows + 1, :] for h in range(QH)]
            + [jnp.zeros((8 - QH, 2 * HD), F32)], axis=0)
        m = mo
        for d in range(nhalf):
            m = jnp.maximum(m, xr[d, :, 0:HD])
        total = ao * wide(jnp.exp2(mo - m), 2)
        for d in range(nhalf):
            total = total + xr[d, :, HD:] * wide(jnp.exp2(xr[d, :, 0:HD] - m), 2)
        for h in range(QH):
            acc[h * half_rows:h * half_rows + 1, :] = total[h:h + 1, :]

    def send_att(r):
        return remote(att.at[r], attp.at[r], ax_s.at[r], ax_r.at[r], across)

    for r in range(2):
        for h in range(QH):
            at = (r * QH + h) * half_rows
            block = acc[at:at + half_rows, :]
            att[r, :, h * HD:(h + 1) * HD] = (block[:, 0:HD] / block[:, HD:]).astype(BF)
        send_att(r).start()

    for j in range(ny):
        own_weights(j).wait()
        passed_weights(j).wait_recv()

    def send_y(r, j):
        return remote(ysb.at[r, j], yrb.at[r, j], y_s.at[r, j], y_r.at[r, j], along_y(j))

    order = sorted(range(1, ny), key=lambda j: -min(j, ny - j))
    for r in range(2):
        send_att(r).wait_recv()
        for j in order + [0]:
            part = dot(att[r], w2[j, 0:width, :]) + dot(attp[r], w2[j, width:, :])
            ysb[r, j] = part.astype(BF)
            if j:
                send_y(r, j).start()

    for r in range(2):
        total = ysb[r, 0].astype(F32)
        for j in order[::-1]:
            send_y(r, j).wait_recv()
            total = total + yrb[r, j].astype(F32)
        out_ref[r * half_rows:(r + 1) * half_rows, :] = total.astype(BF)

    for r in range(2):
        send_att(r).wait_send()
        for j in order:
            send_y(r, j).wait_send()
    for j in range(ny):
        send_weights(j).wait_send()
        pass_weights(j).wait_send()

    def sent(k, carry):
        for i in (1, 0):
            @pl.when(zz < nz - 1)
            def _():
                send_up(own, i, k).wait_send()
            send_peer(own, i, k).wait_send()
        return carry
    lax.fori_loop(0, zz + 1, sent, 0)

    @pl.when(c < nhalf)
    def _():
        send_xp().wait_send()

    @pl.when(c == extra)
    def _():
        def body(d, carry):
            send_xq(d).wait_send()
            return carry
        lax.fori_loop(0, nhalf, body, 0)


def shards(nc, nh, queries, keys_values, offsets, w_out):
    rows = queries.shape[0]
    width = QH * HD
    nhalf = nc // 2
    nz = nhalf // 2
    ny = nh // 2
    half_rows = rows // 2
    dma = pltpu.SemaphoreType.DMA
    vmem = pl.BlockSpec(memory_space=pltpu.VMEM)
    return pl.pallas_call(
        functools.partial(kernel, nc, nh, rows),
        out_shape=jax.ShapeDtypeStruct((rows, width), BF),
        in_specs=[vmem, vmem, pl.BlockSpec(memory_space=pltpu.SMEM), pl.BlockSpec(memory_space=pl.ANY)],
        out_specs=vmem,
        scratch_shapes=[
            pltpu.VMEM((QH * rows, HD), BF),
            pltpu.VMEM((nhalf, 2, rows, HD), BF),
            pltpu.VMEM((rows, HD), jnp.int32),
            pltpu.VMEM((QH * rows, HD), F32),
            pltpu.VMEM((QH * rows, 2 * HD), F32),
            pltpu.VMEM((ny, 2 * width, width), BF),
            pltpu.VMEM((2, half_rows, width), BF),
            pltpu.VMEM((2, half_rows, width), BF),
            pltpu.VMEM((2, ny, half_rows, width), BF),
            pltpu.VMEM((2, ny, half_rows, width), BF),
            pltpu.VMEM((16, HD), BF),
            pltpu.VMEM((8, 3 * HD), F32),
            pltpu.VMEM((nhalf, 8, 3 * HD), F32),
            dma((nz, 2)), dma((nz, 2)), dma((nhalf, 2)),
            dma((ny,)), dma((ny,)), dma((ny,)), dma((ny,)), dma((ny,)),
            dma((2,)), dma((2,)),
            dma((2, ny)), dma((2, ny)),
            dma((nhalf,)), dma, dma, dma((nhalf,)),
        ],
        compiler_params=pltpu.CompilerParams(
            collective_id=0, has_side_effects=True, vmem_limit_bytes=40 * 1024 * 1024),
        cost_estimate=pl.CostEstimate(flops=4 * 10 ** 9, bytes_accessed=6 * 2 ** 20, transcendentals=4 * 2 ** 20),
    )(queries, keys_values, offsets, w_out)


def solution(mesh):
    nc, nh = mesh.shape["ctx"], mesh.shape["head"]

    def program(queries, keys_values, positions, offsets, w_out):
        return shards(nc, nh, queries, keys_values, offsets, w_out)

    in_specs = (
        P(("dp", "ctx"), "head"),
        P(None, ("dp", "ctx"), "head"),
        P(("dp", "ctx")),
        P("dp"),
        P("head", None),
    )
    out_specs = P(("dp", "ctx"), "head")
    return jax.shard_map(program, mesh=mesh, in_specs=in_specs, out_specs=out_specs, check_vma=False)
```

```python
import functools
import math

import jax
import jax.numpy as jnp
from jax import lax
from jax.experimental import pallas as pl
from jax.experimental.pallas import tpu as pltpu
from jax.sharding import PartitionSpec as P

HD = 128
QH = 4
NR = 4
ROPE_BASE = 500000.0
STRETCH = 16.0
ANCHOR_LENGTH = 8192.0
BETA_FAST = 32.0
BETA_SLOW = 1.0
MAGNITUDE = 0.1 * math.log(16.0) + 1.0
NEGATIVE = -1e30
LOG2E = 1.4426950408889634
MESH = pl.DeviceIdType.MESH
BF = jnp.bfloat16
F32 = jnp.float32


def remote(src, dst, send_sem, recv_sem, device):
    return pltpu.make_async_remote_copy(
        src_ref=src, dst_ref=dst, send_sem=send_sem, recv_sem=recv_sem,
        device_id=device, device_id_type=MESH,
    )


def dot(a, b):
    return jnp.dot(a, b, preferred_element_type=F32)


def dot_t(a, b):
    return lax.dot_general(a, b, (((1,), (1,)), ((), ())), preferred_element_type=F32)


def kernel(
    nc, nh, rows,
    q_hbm, kv_hbm, off_hbm, w_ref, out_ref,
    q_ref, kv_ref, off_ref, in_s,
    qs, kvb, st, mx, acc, w2, att, attp, ysb, rlb, yrb, outb, xq, xp, xr,
    up_s, peer_s, kv_r, wl_s, ws_s, wr_s, wf_s, wf_r, ax_s, ax_r, rl_s, rl_r, yd_s, yd_r, ys_s, ys_r, out_s, go, xq_s, xq_r, xr_s, xr_r,
):
    nhalf = nc // 2
    nz = nhalf // 2
    ny = nh // 2
    part = rows // NR
    mrows = QH * part
    width = QH * HD
    wrows = width // 2
    hw = width // 2

    c = lax.axis_index("ctx")
    hd = lax.axis_index("head")
    dp = lax.axis_index("dp")
    z = c // 2
    core = c % 2
    half = z // nz
    zz = z % nz
    own = 2 * zz + core
    other = 2 * zz + 1 - core
    y = hd // 2
    x = hd % 2
    up = {"ctx": jnp.minimum(c + 2, nc - 1)}
    down = {"ctx": jnp.maximum(c - 2, 0)}
    peer = {"ctx": c + 1 - 2 * core}
    across = {"head": hd + 1 - 2 * x}
    same_dp = x == core
    w_to = {"head": hd + 1 - 2 * x, "dp": jnp.where(same_dp, dp, 1 - dp)}
    w_from = {"head": hd + 1 - 2 * x, "dp": jnp.where(same_dp, 1 - dp, dp)}
    extra = nhalf

    def along_y(j):
        return {"head": ((y + j) % ny) * 2 + x}

    barrier = pltpu.get_barrier_semaphore()

    def greet(device):
        pl.semaphore_signal(barrier, inc=1, device_id=device, device_id_type=MESH)

    greet(peer)
    greet(across)
    greet(w_to)
    greet(w_from)
    for j in range(1, ny):
        greet(along_y(j))

    @pl.when(zz < nz - 1)
    def _():
        greet(up)

    @pl.when(zz > 0)
    def _():
        greet(down)

    @pl.when(c < nhalf)
    def _():
        greet({"ctx": jnp.int32(extra)})

    def own_weights(j):
        col = pl.multiple_of((((y + j) % ny) * 2 + x) * width, 128)
        return pltpu.make_async_copy(
            w_ref.at[:, pl.ds(col, width)], w2.at[j, pl.ds(0, width), :], wl_s.at[j])

    offsets_in = pltpu.make_async_copy(off_hbm, off_ref, in_s.at[0])
    keys_in = pltpu.make_async_copy(kv_hbm, kv_ref, in_s.at[1])
    queries_in = pltpu.make_async_copy(q_hbm, q_ref, in_s.at[2])
    offsets_in.start()
    keys_in.start()
    queries_in.start()
    for j in range(ny):
        own_weights(j).start()

    lane = lax.broadcasted_iota(jnp.int32, (rows, HD), 1)
    token = lax.broadcasted_iota(jnp.int32, (rows, HD), 0) + c * rows
    start = jnp.zeros((rows, HD), jnp.int32)
    offsets_in.wait()
    for d in range(off_ref.shape[0]):
        o = off_ref[d]
        start = jnp.maximum(start, jnp.where(token >= o, o, 0))
    st[...] = start
    index = (lax.broadcasted_iota(jnp.int32, (8, HD), 1) % (HD // 2)).astype(F32)
    base = jnp.exp(index * (-2.0 * math.log(ROPE_BASE) / HD))
    ramp = jnp.clip((base * (ANCHOR_LENGTH / (2.0 * math.pi)) - BETA_SLOW) / (BETA_FAST - BETA_SLOW), 0.0, 1.0)
    freq = base * (1.0 - ramp) / STRETCH + base * ramp
    angle = (token - start).astype(F32) * freq[0:1]
    cosine = jnp.cos(angle) * MAGNITUDE
    sine = jnp.sin(angle) * jnp.where(lane < HD // 2, -MAGNITUDE, MAGNITUDE)

    def rotate(field):
        field = field.astype(F32)
        return field * cosine + pltpu.roll(field, HD // 2, 1) * sine

    keys_in.wait()
    kvb[own, 1] = kv_ref[1]
    kvb[own, 0] = rotate(kv_ref[0]).astype(BF)

    @pl.when(c != extra)
    def _():
        pl.semaphore_wait(barrier, 4 + (ny - 1) + jnp.where(zz < nz - 1, 1, 0) + jnp.where(zz > 0, 1, 0))

    @pl.when(c == extra + 1)
    def _():
        pl.semaphore_signal(go, inc=1, device_id=peer, device_id_type=MESH)

    if nz > 1:
        @pl.when(c == extra + 2)
        def _():
            pl.semaphore_signal(go, inc=1, device_id=down, device_id_type=MESH)

    @pl.when(c == extra)
    def _():
        pl.semaphore_wait(go, 2 if nz > 1 else 1)

    def send_up(slot, i, step):
        return remote(kvb.at[slot, i], kvb.at[slot, i], up_s.at[step, i], kv_r.at[slot, i], up)

    def send_peer(slot, i, step):
        return remote(kvb.at[slot, i], kvb.at[slot, i], peer_s.at[step, i], kv_r.at[slot, i], peer)

    @pl.when(zz < nz - 1)
    def _():
        for i in (1, 0):
            send_up(own, i, 0).start()
    for i in (1, 0):
        send_peer(own, i, 0).start()

    @pl.when(c == extra)
    def _():
        pl.semaphore_wait(barrier, 4 + (ny - 1) + nhalf + (1 if nz > 1 else 0))

    wrow = pl.multiple_of(core * wrows, 128)
    wback = pl.multiple_of((1 - core) * wrows, 128)

    def send_weights(j):
        col = pl.multiple_of((((y + j) % ny) * 2 + 1 - x) * width, 128)
        return remote(
            w_ref.at[pl.ds(wrow, wrows), pl.ds(col, width)],
            w2.at[j, pl.ds(width + wrow, wrows), :], ws_s.at[j], wr_s.at[j], w_to)

    def pass_weights(j):
        at = w2.at[j, pl.ds(width + wrow, wrows), :]
        return remote(at, at, wf_s.at[j], wf_r.at[j], peer)

    def passed_weights(j):
        at = w2.at[j, pl.ds(width + wback, wrows), :]
        return remote(at, at, wf_s.at[j], wf_r.at[j], peer)

    for j in range(ny):
        send_weights(j).start()

    def forward_weights():
        for j in range(ny):
            send_weights(j).wait_recv()
            pass_weights(j).start()

    scale = HD ** (-0.5) * LOG2E
    queries_in.wait()
    for h in range(QH):
        rot = (rotate(q_ref[:, h * HD:(h + 1) * HD]) * scale).astype(BF)
        for r in range(NR):
            at = r * mrows + h * part
            qs[at:at + part, :] = rot[r * part:(r + 1) * part]

    def send_xq(d):
        return remote(xq, xq, xq_s.at[d], xq_r, {"ctx": d})

    @pl.when(c == extra)
    def _():
        heads = [qs[h * part:h * part + 1, :] for h in range(QH)]
        xq[...] = jnp.concatenate(heads + [jnp.zeros((16 - QH, HD), BF)], axis=0)

        def body(d, carry):
            send_xq(d).start()
            return carry
        lax.fori_loop(0, nhalf, body, 0)

    def with_ones(v):
        return jnp.concatenate([v, jnp.ones(v.shape, BF)], axis=1)

    def wide(v, n):
        return jnp.tile(v, (1, n))

    def starts_of(t):
        return jnp.concatenate([st[t * part:(t + 1) * part, :]] * QH, axis=0)

    def tokens_of(t, n):
        i = lax.broadcasted_iota(jnp.int32, (mrows, n), 0) % part
        return i + (c * rows + t * part)

    for t in range(NR):
        at = slice(t * mrows, (t + 1) * mrows)
        s = dot_t(qs[at, :], kvb[own, 0])
        key = lax.broadcasted_iota(jnp.int32, (mrows, rows), 1) + c * rows
        seen = (key <= tokens_of(t, rows)) & (key >= wide(starts_of(t), rows // HD))
        s = jnp.where(seen, s, NEGATIVE)
        m = jnp.broadcast_to(jnp.max(s, axis=1, keepdims=True), (mrows, HD))
        p = jnp.exp2(s - wide(m, rows // HD)).astype(BF)
        mx[at, :] = m
        acc[at, :] = dot(p, with_ones(kvb[own, 1]))

    def update(first, keys, values, masked, tiles=range(NR)):
        n = keys.shape[0]
        values = with_ones(values)
        for t in tiles:
            at = slice(t * mrows, (t + 1) * mrows)
            s = dot_t(qs[at, :], keys)
            if masked:
                key = lax.broadcasted_iota(jnp.int32, (mrows, n), 1) + first
                s = jnp.where(key >= wide(starts_of(t), n // HD), s, NEGATIVE)
            before = mx[at, :]
            m = jnp.maximum(before, jnp.max(s, axis=1, keepdims=True))
            p = jnp.exp2(s - wide(m, n // HD)).astype(BF)
            alpha = jnp.exp2(before - m)
            mx[at, :] = m
            acc[at, :] = acc[at, :] * wide(alpha, 2) + dot(p, values)

    def send_xp():
        return remote(xp, xr.at[own], xr_s, xr_r.at[own], {"ctx": jnp.int32(extra)})

    def shared_token():
        send_xq(0).wait_recv()
        s = dot_t(xq[...], kvb[own, 0])
        m = jnp.broadcast_to(jnp.max(s, axis=1, keepdims=True), (16, HD))
        p = jnp.exp2(s - wide(m, rows // HD)).astype(BF)
        xp[:, 0:HD] = m[0:8]
        xp[:, HD:] = dot(p, with_ones(kvb[own, 1]))[0:8]
        send_xp().start()

    for i in (1, 0):
        send_peer(other, i, 0).wait_recv()

    @pl.when(core == 1)
    def _():
        update((c - 1) * rows, kvb[other, 0], kvb[other, 1], True)

    late = min(5, nz - 1)
    asked = min(2, nz - 1)

    def both(chip):
        for i in (1, 0):
            send_peer(2 * chip + 1 - core, i, 0).wait_recv()
        keys = jnp.concatenate([kvb[2 * chip, 0], kvb[2 * chip + 1, 0]], axis=0)
        values = jnp.concatenate([kvb[2 * chip, 1], kvb[2 * chip + 1, 1]], axis=0)

        @pl.when(half == 0)
        def _():
            update(0, keys, values, False)

        @pl.when(half == 1)
        def _():
            update((half * nhalf + 2 * chip) * rows, keys, values, True)

    def step(k, carry):
        mine = 2 * (zz - k) + core
        for i in (1, 0):
            send_up(mine, i, 0).wait_recv()

            @pl.when(zz < nz - 1)
            def _():
                send_up(mine, i, k).start()
            send_peer(mine, i, k).start()

        @pl.when(k > 1)
        def _():
            both(zz - k + 1)

        @pl.when((k == asked) & (c < nhalf))
        def _():
            shared_token()

        @pl.when(k == late)
        def _():
            forward_weights()
        return carry

    lax.fori_loop(1, zz + 1, step, 0)

    @pl.when((zz < asked) & (c < nhalf))
    def _():
        shared_token()

    @pl.when(zz < late)
    def _():
        forward_weights()

    @pl.when(c == extra)
    def _():
        def arrived(d, carry):
            remote(xp, xr.at[d], xr_s, xr_r.at[d], {"ctx": jnp.int32(0)}).wait_recv()
            return carry
        lax.fori_loop(0, nhalf, arrived, 0)
        pad = [jnp.zeros((8 - QH, HD), F32)]
        mo = jnp.concatenate([mx[h * part:h * part + 1, :] for h in range(QH)] + pad, axis=0)
        ao = jnp.concatenate(
            [acc[h * part:h * part + 1, :] for h in range(QH)]
            + [jnp.zeros((8 - QH, 2 * HD), F32)], axis=0)
        m = mo
        for d in range(nhalf):
            m = jnp.maximum(m, xr[d, :, 0:HD])
        total = ao * wide(jnp.exp2(mo - m), 2)
        for d in range(nhalf):
            total = total + xr[d, :, HD:] * wide(jnp.exp2(xr[d, :, 0:HD] - m), 2)
        for h in range(QH):
            acc[h * part:h * part + 1, :] = total[h:h + 1, :]

    def send_att(r):
        return remote(att.at[r], attp.at[r], ax_s.at[r], ax_r.at[r], across)

    def last(slot, tiles):
        @pl.when((zz > 0) & (half == 0))
        def _():
            update(0, kvb[slot, 0], kvb[slot, 1], False, tiles)

        @pl.when((zz > 0) & (half == 1))
        def _():
            update((half * nhalf + slot) * rows, kvb[slot, 0], kvb[slot, 1], True, tiles)

    last(core, range(NR))

    @pl.when(zz > 0)
    def _():
        for i in (1, 0):
            send_peer(1 - core, i, 0).wait_recv()

    for r in range(NR):
        last(1 - core, [r])
        for h in range(QH):
            at = r * mrows + h * part
            block = acc[at:at + part, :]
            att[r, :, h * HD:(h + 1) * HD] = (block[:, 0:HD] / block[:, HD:]).astype(BF)
        send_att(r).start()

    for j in range(ny):
        own_weights(j).wait()
        passed_weights(j).wait_recv()

    low, high = pl.ds(0, hw), pl.ds(hw, hw)
    ahead, back = along_y(1), along_y(ny - 1)

    def relay(r, way):
        cols, to = ((low, ahead), (high, back))[way]
        return remote(ysb.at[r, 2, :, cols], rlb.at[r, way], rl_s.at[r, way], rl_r.at[r, way], to)

    def direct(r, way):
        cols, to = ((high, ahead), (low, back))[way]
        j = (1, 3)[way]
        return remote(ysb.at[r, j, :, cols], yrb.at[r, way, :, cols], yd_s.at[r, way], yd_r.at[r, way], to)

    def summed(r, way):
        cols, to = ((low, ahead), (high, back))[way]
        j = (1, 3)[way]
        return remote(ysb.at[r, j, :, cols], yrb.at[r, way, :, cols], ys_s.at[r, way], ys_r.at[r, way], to)

    def join(r):
        for way in range(2):
            relay(r, way).wait_recv()
            j = (1, 3)[way]
            at = slice(way * hw, (way + 1) * hw)
            ysb[r, j, :, at] = (ysb[r, j, :, at].astype(F32) + rlb[r, way].astype(F32)).astype(BF)
            summed(r, way).start()

    def write(r):
        return pltpu.make_async_copy(outb.at[r], out_ref.at[pl.ds(r * part, part), :], out_s.at[r])

    def total(r):
        result = ysb[r, 0].astype(F32)
        for way in range(2):
            direct(r, way).wait_recv()
            summed(r, way).wait_recv()
            result = result + yrb[r, way].astype(F32)
        outb[r] = result.astype(BF)
        write(r).start()

    for r in range(NR):
        send_att(r).wait_recv()
        for j in (2, 1, 3, 0):
            value = dot(att[r], w2[j, 0:width, :]) + dot(attp[r], w2[j, width:, :])
            ysb[r, j] = value.astype(BF)
            if j == 2:
                relay(r, 0).start()
                relay(r, 1).start()
            elif j:
                direct(r, j // 2).start()
        if r:
            join(r - 1)
    join(NR - 1)
    for r in range(NR):
        total(r)

    for r in range(NR):
        write(r).wait()
        send_att(r).wait_send()
        for way in range(2):
            relay(r, way).wait_send()
            direct(r, way).wait_send()
            summed(r, way).wait_send()
    for j in range(ny):
        send_weights(j).wait_send()
        pass_weights(j).wait_send()

    def sent(k, carry):
        for i in (1, 0):
            @pl.when(zz < nz - 1)
            def _():
                send_up(own, i, k).wait_send()
            send_peer(own, i, k).wait_send()
        return carry
    lax.fori_loop(0, zz + 1, sent, 0)

    @pl.when(c < nhalf)
    def _():
        send_xp().wait_send()

    @pl.when(c == extra)
    def _():
        def body(d, carry):
            send_xq(d).wait_send()
            return carry
        lax.fori_loop(0, nhalf, body, 0)


def shards(nc, nh, queries, keys_values, offsets, w_out):
    rows = queries.shape[0]
    width = QH * HD
    nhalf = nc // 2
    nz = nhalf // 2
    ny = nh // 2
    part = rows // NR
    dma = pltpu.SemaphoreType.DMA
    return pl.pallas_call(
        functools.partial(kernel, nc, nh, rows),
        out_shape=jax.ShapeDtypeStruct((rows, width), BF),
        in_specs=[pl.BlockSpec(memory_space=pl.ANY)] * 4,
        out_specs=pl.BlockSpec(memory_space=pl.ANY),
        scratch_shapes=[
            pltpu.VMEM(queries.shape, BF),
            pltpu.VMEM(keys_values.shape, BF),
            pltpu.SMEM(offsets.shape, jnp.int32),
            dma((3,)),
            pltpu.VMEM((QH * rows, HD), BF),
            pltpu.VMEM((nhalf, 2, rows, HD), BF),
            pltpu.VMEM((rows, HD), jnp.int32),
            pltpu.VMEM((QH * rows, HD), F32),
            pltpu.VMEM((QH * rows, 2 * HD), F32),
            pltpu.VMEM((ny, 2 * width, width), BF),
            pltpu.VMEM((NR, part, width), BF),
            pltpu.VMEM((NR, part, width), BF),
            pltpu.VMEM((NR, ny, part, width), BF),
            pltpu.VMEM((NR, 2, part, width // 2), BF),
            pltpu.VMEM((NR, 2, part, width), BF),
            pltpu.VMEM((NR, part, width), BF),
            pltpu.VMEM((16, HD), BF),
            pltpu.VMEM((8, 3 * HD), F32),
            pltpu.VMEM((nhalf, 8, 3 * HD), F32),
            dma((nz, 2)), dma((nz, 2)), dma((nhalf, 2)),
            dma((ny,)), dma((ny,)), dma((ny,)), dma((ny,)), dma((ny,)),
            dma((NR,)), dma((NR,)),
            dma((NR, 2)), dma((NR, 2)), dma((NR, 2)),
            dma((NR, 2)), dma((NR, 2)), dma((NR, 2)),
            dma((NR,)), pltpu.SemaphoreType.REGULAR,
            dma((nhalf,)), dma, dma, dma((nhalf,)),
        ],
        compiler_params=pltpu.CompilerParams(
            collective_id=0, has_side_effects=True, vmem_limit_bytes=60 * 1024 * 1024),
        cost_estimate=pl.CostEstimate(flops=4 * 10 ** 9, bytes_accessed=6 * 2 ** 20, transcendentals=4 * 2 ** 20),
    )(queries, keys_values, offsets, w_out)


def solution(mesh):
    nc, nh = mesh.shape["ctx"], mesh.shape["head"]

    def program(queries, keys_values, positions, offsets, w_out):
        return shards(nc, nh, queries, keys_values, offsets, w_out)

    in_specs = (
        P(("dp", "ctx"), "head"),
        P(None, ("dp", "ctx"), "head"),
        P(("dp", "ctx")),
        P("dp"),
        P("head", None),
    )
    out_specs = P(("dp", "ctx"), "head")
    return jax.shard_map(program, mesh=mesh, in_specs=in_specs, out_specs=out_specs, check_vma=False)
```

```python
import functools
import math

import jax
import jax.numpy as jnp
from jax import lax
from jax.experimental import pallas as pl
from jax.experimental.pallas import tpu as pltpu
from jax.sharding import PartitionSpec as P

HD = 128
QH = 4
NR = 2
ORDER = (2, 1, 3, 0)
ROPE_BASE = 500000.0
STRETCH = 16.0
ANCHOR_LENGTH = 8192.0
BETA_FAST = 32.0
BETA_SLOW = 1.0
MAGNITUDE = 0.1 * math.log(16.0) + 1.0
NEGATIVE = -1e30
LOG2E = 1.4426950408889634
MESH = pl.DeviceIdType.MESH
BF = jnp.bfloat16
F32 = jnp.float32


def remote(src, dst, send_sem, recv_sem, device):
    return pltpu.make_async_remote_copy(
        src_ref=src, dst_ref=dst, send_sem=send_sem, recv_sem=recv_sem,
        device_id=device, device_id_type=MESH,
    )


def dot(a, b):
    return jnp.dot(a, b, preferred_element_type=F32)


def dot_t(a, b):
    return lax.dot_general(a, b, (((1,), (1,)), ((), ())), preferred_element_type=F32)


def kernel(
    nc, nh, rows,
    q_hbm, kv_hbm, off_hbm, w_ref, own_ref, ahead_ref, back_ref,
    q_ref, k_ref, off_ref, in_s,
    qs, kvb, st, mx, acc, w2, att, attp, half_sum, ysb, rlb, pas, xq, xp, xr,
    up_s, peer_s, kv_r, wl_s, ws_s, wr_s, wf_s, wf_r, ax_s, ax_r, rl_s, rl_r, yd_s, yd_r, ys_s, ys_r, out_s, go, f1_s, f1_r, f2_s, xq_s, xq_r, xr_s, xr_r,
):
    nhalf = nc // 2
    nz = nhalf // 2
    ny = nh // 2
    part = rows // NR
    mrows = QH * part
    width = QH * HD
    wrows = width // 2
    hw = width // 2

    c = lax.axis_index("ctx")
    hd = lax.axis_index("head")
    dp = lax.axis_index("dp")
    z = c // 2
    core = c % 2
    half = z // nz
    zz = z % nz
    own = 2 * zz + core
    other = 2 * zz + 1 - core
    y = hd // 2
    x = hd % 2
    up = {"ctx": jnp.minimum(c + 2, nc - 1)}
    down = {"ctx": jnp.maximum(c - 2, 0)}
    peer = {"ctx": c + 1 - 2 * core}
    across = {"head": hd + 1 - 2 * x}
    same_dp = x == core
    w_to = {"head": hd + 1 - 2 * x, "dp": jnp.where(same_dp, dp, 1 - dp)}
    w_from = {"head": hd + 1 - 2 * x, "dp": jnp.where(same_dp, 1 - dp, dp)}
    extra = nhalf
    dist = nhalf - 1
    token = jnp.where(c == extra, 1, 0) + jnp.where(c == dist, nhalf - 1, 0)

    def along_y(j):
        return {"head": ((y + j) % ny) * 2 + x}

    barrier = pltpu.get_barrier_semaphore()

    wrap = nz == 8
    up_steps = jnp.where(half == 1, nz - 2, nz - 1) if wrap else nz - 1
    relay_at = 2 * (nz - 2)
    source = (half == 1) & (zz == 0)
    sink = (half == 1) & (zz == nz - 1)
    far = jnp.where(source, 1, 0)

    def greet(device):
        pl.semaphore_signal(barrier, inc=1, device_id=device, device_id_type=MESH)

    greet(peer)
    greet(across)
    greet(w_to)
    greet(w_from)
    for j in range(1, ny):
        greet(along_y(j))

    @pl.when(zz < nz - 1)
    def _():
        greet(up)

    @pl.when(zz > 0)
    def _():
        greet(down)

    @pl.when(c < dist)
    def _():
        greet({"ctx": jnp.int32(dist)})

    @pl.when(c == dist)
    def _():
        greet({"ctx": jnp.int32(extra)})

    if wrap:
        @pl.when(c == relay_at)
        def _():
            for column in range(2):
                greet({"ctx": jnp.int32(nhalf + column)})

        @pl.when(sink)
        def _():
            greet({"ctx": jnp.int32(relay_at)})

    order = [j for j in ORDER if j < ny]

    def own_weights(j):
        col = pl.multiple_of((((y + j) % ny) * 2 + x) * width, 128)
        return pltpu.make_async_copy(
            w_ref.at[:, pl.ds(col, width)], w2.at[j, pl.ds(0, width), :], wl_s.at[j])

    offsets_in = pltpu.make_async_copy(off_hbm, off_ref, in_s.at[0])
    keys_in = pltpu.make_async_copy(kv_hbm.at[0], k_ref, in_s.at[1])
    values_in = pltpu.make_async_copy(kv_hbm.at[1], kvb.at[own, 1], in_s.at[3])
    queries_in = pltpu.make_async_copy(q_hbm, q_ref, in_s.at[2])
    values_in.start()
    offsets_in.start()
    keys_in.start()
    queries_in.start()
    for j in range(ny):
        own_weights(j).start()

    near = 4 + (ny - 1) + token + jnp.where(zz < nz - 1, 1, 0) + jnp.where(zz > 0, 1, 0)
    if wrap:
        @pl.when(c != relay_at)
        def _():
            pl.semaphore_wait(barrier, near + far)

        @pl.when(c == relay_at + 1)
        def _():
            pl.semaphore_signal(go, inc=1, device_id=peer, device_id_type=MESH)

        @pl.when(c == relay_at + 2)
        def _():
            pl.semaphore_signal(go, inc=1, device_id=down, device_id_type=MESH)

        @pl.when(c == relay_at)
        def _():
            pl.semaphore_wait(go, 2)
    else:
        pl.semaphore_wait(barrier, near)

    def send_up(slot, i, step):
        return remote(kvb.at[slot, i], kvb.at[slot, i], up_s.at[step, i], kv_r.at[slot, i], up)

    def send_peer(slot, i, step):
        return remote(kvb.at[slot, i], kvb.at[slot, i], peer_s.at[step, i], kv_r.at[slot, i], peer)

    def send_own(i):
        @pl.when(zz < nz - 1)
        def _():
            send_up(own, i, 0).start()

        if wrap:
            for column in range(2):
                @pl.when(source & (core == column))
                def _():
                    first_leg(i, column).start()

        @pl.when(core == 0)
        def _():
            send_peer(own, i, 0).start()

    def first_leg(i, column):
        return remote(kvb.at[own, i], pas.at[column, i], f1_s.at[i], f1_r.at[column, i], {"ctx": jnp.int32(relay_at)})

    def second_leg(i, column):
        return remote(
            pas.at[column, i], kvb.at[column, i], f2_s.at[column, i], kv_r.at[column, i],
            {"ctx": jnp.int32(nhalf + 2 * (nz - 1) + column)})

    values_in.wait()
    send_own(1)

    lane = lax.broadcasted_iota(jnp.int32, (rows, HD), 1)
    token = lax.broadcasted_iota(jnp.int32, (rows, HD), 0) + c * rows
    start = jnp.zeros((rows, HD), jnp.int32)
    offsets_in.wait()
    for d in range(off_ref.shape[0]):
        o = off_ref[d]
        start = jnp.maximum(start, jnp.where(token >= o, o, 0))
    st[...] = start
    index = (lax.broadcasted_iota(jnp.int32, (8, HD), 1) % (HD // 2)).astype(F32)
    base = jnp.exp(index * (-2.0 * math.log(ROPE_BASE) / HD))
    ramp = jnp.clip((base * (ANCHOR_LENGTH / (2.0 * math.pi)) - BETA_SLOW) / (BETA_FAST - BETA_SLOW), 0.0, 1.0)
    freq = base * (1.0 - ramp) / STRETCH + base * ramp
    angle = (token - start).astype(F32) * freq[0:1]
    cosine = jnp.cos(angle) * MAGNITUDE
    sine = jnp.sin(angle) * jnp.where(lane < HD // 2, -MAGNITUDE, MAGNITUDE)

    def rotate(field):
        field = field.astype(F32)
        return field * cosine + pltpu.roll(field, HD // 2, 1) * sine

    keys_in.wait()
    kvb[own, 0] = rotate(k_ref[...]).astype(BF)
    send_own(0)

    if wrap:
        @pl.when(c == relay_at)
        def _():
            pl.semaphore_wait(barrier, near + 2)

    wrow = pl.multiple_of(core * wrows, 128)
    wback = pl.multiple_of((1 - core) * wrows, 128)

    def send_weights(j):
        col = pl.multiple_of((((y + j) % ny) * 2 + 1 - x) * width, 128)
        return remote(
            w_ref.at[pl.ds(wrow, wrows), pl.ds(col, width)],
            w2.at[j, pl.ds(width + wrow, wrows), :], ws_s.at[j], wr_s.at[j], w_to)

    def pass_weights(j):
        at = w2.at[j, pl.ds(width + wrow, wrows), :]
        return remote(at, at, wf_s.at[j], wf_r.at[j], peer)

    def passed_weights(j):
        at = w2.at[j, pl.ds(width + wback, wrows), :]
        return remote(at, at, wf_s.at[j], wf_r.at[j], peer)

    for j in order:
        send_weights(j).start()

    def forward_weights(j):
        send_weights(j).wait_recv()
        pass_weights(j).start()

    scale = HD ** (-0.5) * LOG2E
    queries_in.wait()
    for h in range(QH):
        rot = (rotate(q_ref[:, h * HD:(h + 1) * HD]) * scale).astype(BF)
        for r in range(NR):
            at = r * mrows + h * part
            qs[at:at + part, :] = rot[r * part:(r + 1) * part]

    def hand_over():
        return remote(xq, xq, xq_s.at[0], xq_r, {"ctx": jnp.int32(dist)})

    def hand_out(d):
        return remote(xq, xq, xq_s.at[d], xq_r, {"ctx": d})

    @pl.when(c == extra)
    def _():
        heads = [qs[h * part:h * part + 1, :] for h in range(QH)]
        xq[...] = jnp.concatenate(heads + [jnp.zeros((16 - QH, HD), BF)], axis=0)
        hand_over().start()

    @pl.when(c == dist)
    def _():
        hand_out(0).wait_recv()

        def body(d, carry):
            hand_out(d).start()
            return carry
        lax.fori_loop(0, nhalf - 1, body, 0)

    def with_ones(v):
        return jnp.concatenate([v, jnp.ones(v.shape, BF)], axis=1)

    def wide(v, n):
        return jnp.tile(v, (1, n))

    def starts_of(t):
        return jnp.concatenate([st[t * part:(t + 1) * part, :]] * QH, axis=0)

    def tokens_of(t, n):
        i = lax.broadcasted_iota(jnp.int32, (mrows, n), 0) % part
        return i + (c * rows + t * part)

    for t in range(NR):
        at = slice(t * mrows, (t + 1) * mrows)
        s = dot_t(qs[at, :], kvb[own, 0])
        key = lax.broadcasted_iota(jnp.int32, (mrows, rows), 1) + c * rows
        seen = (key <= tokens_of(t, rows)) & (key >= wide(starts_of(t), rows // HD))
        s = jnp.where(seen, s, NEGATIVE)
        m = jnp.broadcast_to(jnp.max(s, axis=1, keepdims=True), (mrows, HD))
        p = jnp.exp2(s - wide(m, rows // HD)).astype(BF)
        mx[at, :] = m
        acc[at, :] = dot(p, with_ones(kvb[own, 1]))

    def update(first, keys, values, masked, tiles=range(NR)):
        n = keys.shape[0]
        values = with_ones(values)
        for t in tiles:
            at = slice(t * mrows, (t + 1) * mrows)
            s = dot_t(qs[at, :], keys)
            if masked:
                key = lax.broadcasted_iota(jnp.int32, (mrows, n), 1) + first
                s = jnp.where(key >= wide(starts_of(t), n // HD), s, NEGATIVE)
            before = mx[at, :]
            m = jnp.maximum(before, jnp.max(s, axis=1, keepdims=True))
            p = jnp.exp2(s - wide(m, n // HD)).astype(BF)
            alpha = jnp.exp2(before - m)
            mx[at, :] = m
            acc[at, :] = acc[at, :] * wide(alpha, 2) + dot(p, values)

    def send_xp():
        return remote(xp, xr.at[own], xr_s, xr_r.at[own], {"ctx": jnp.int32(extra)})

    def answer_token():
        @pl.when(c != dist)
        def _():
            hand_over().wait_recv()

        s = dot_t(xq[...], kvb[own, 0])
        m = jnp.broadcast_to(jnp.max(s, axis=1, keepdims=True), (16, HD))
        p = jnp.exp2(s - wide(m, rows // HD)).astype(BF)
        sums = dot(p, with_ones(kvb[own, 1]))
        xp[0:QH, :] = sums[0:QH, 0:HD]
        xp[QH:2 * QH, :] = jnp.where(lane[0:QH] < HD // 2, m[0:QH], sums[0:QH, HD:])
        send_xp().start()

    @pl.when(core == 1)
    def _():
        for i in (1, 0):
            send_peer(other, i, 0).wait_recv()
        update((c - 1) * rows, kvb[other, 0], kvb[other, 1], True)

    steps = jnp.minimum(zz, up_steps)

    def both(chip):
        for i in (1, 0):
            send_peer(2 * chip + 1 - core, i, 0).wait_recv()
        keys = jnp.concatenate([kvb[2 * chip, 0], kvb[2 * chip + 1, 0]], axis=0)
        values = jnp.concatenate([kvb[2 * chip, 1], kvb[2 * chip + 1, 1]], axis=0)

        @pl.when(half == 0)
        def _():
            update(0, keys, values, False)

        @pl.when(half == 1)
        def _():
            update((half * nhalf + 2 * chip) * rows, keys, values, True)

    def step(k, carry):
        mine = 2 * (zz - k) + core
        for i in (1, 0):
            send_up(mine, i, 0).wait_recv()

            @pl.when((zz < nz - 1) & (k < up_steps))
            def _():
                send_up(mine, i, k).start()
            send_peer(mine, i, k).start()

        @pl.when(k > 1)
        def _():
            both(zz - k + 1)

        @pl.when((k == 3) & (zz > 3) & (c < nhalf))
        def _():
            answer_token()

        for i, j in enumerate(order):
            @pl.when(k == i + 2)
            def _():
                forward_weights(j)

        if wrap:
            @pl.when(sink & (k == nz - 3))
            def _():
                for i in (1, 0):
                    send_peer(core, i, 0).wait_recv()
                    send_peer(core, i, nz - 1).start()

            @pl.when((c == relay_at) & (k == 2))
            def _():
                for column in range(2):
                    for i in (1, 0):
                        first_leg(i, column).wait_recv()
                        second_leg(i, column).start()
        return carry

    lax.fori_loop(1, steps + 1, step, 0)

    @pl.when((zz <= 3) & (c < nhalf))
    def _():
        answer_token()

    for i, j in enumerate(order):
        @pl.when(steps < i + 2)
        def _():
            forward_weights(j)

    if wrap:
        @pl.when(sink)
        def _():
            both(zz - up_steps)

    @pl.when(c == extra)
    def _():
        def arrived(d, carry):
            remote(xp, xr.at[d], xr_s, xr_r.at[d], {"ctx": jnp.int32(0)}).wait_recv()
            return carry
        lax.fori_loop(0, nhalf, arrived, 0)
        mo = jnp.concatenate([mx[h * part:h * part + 1, :] for h in range(QH)], axis=0)
        ao = jnp.concatenate([acc[h * part:h * part + 1, :] for h in range(QH)], axis=0)
        tops = [jnp.broadcast_to(xr[d, QH:2 * QH, 0:1], (QH, HD)) for d in range(nhalf)]
        m = functools.reduce(jnp.maximum, tops, mo)
        total = ao * wide(jnp.exp2(mo - m), 2)
        for d in range(nhalf):
            weight = jnp.broadcast_to(xr[d, QH:2 * QH, HD // 2:HD // 2 + 1], (QH, HD))
            total = total + jnp.concatenate([xr[d, 0:QH, :], weight], axis=1) * wide(jnp.exp2(tops[d] - m), 2)
        for h in range(QH):
            acc[h * part:h * part + 1, :] = total[h:h + 1, :]

    def send_att(r):
        return remote(att.at[r], attp.at[r], ax_s.at[r], ax_r.at[r], across)

    def last(slot, tiles):
        @pl.when((zz > 0) & (half == 0))
        def _():
            update(0, kvb[slot, 0], kvb[slot, 1], False, tiles)

        @pl.when((zz > 0) & (half == 1))
        def _():
            update((half * nhalf + slot) * rows, kvb[slot, 0], kvb[slot, 1], True, tiles)

    last(core, range(NR))

    @pl.when(zz > 0)
    def _():
        for i in (1, 0):
            send_peer(1 - core, i, 0).wait_recv()

    for r in range(NR):
        last(1 - core, [r])
        for h in range(QH):
            at = r * mrows + h * part
            block = acc[at:at + part, :]
            att[r, :, h * HD:(h + 1) * HD] = (block[:, 0:HD] / block[:, HD:]).astype(BF)
        send_att(r).start()

    for j in order:
        own_weights(j).wait()
        half_sum[j] = dot(att[...].reshape(rows, width), w2[j, 0:width, :])
    for j in order:
        passed_weights(j).wait_recv()

    low, high = pl.ds(0, hw), pl.ds(hw, hw)
    ahead, back = along_y(1), along_y(ny - 1)

    def relay(r, way):
        cols, to = ((low, ahead), (high, back))[way]
        return remote(ysb.at[r, 2, :, cols], rlb.at[r, way], rl_s.at[r, way], rl_r.at[r, way], to)

    def landing(r, way, cols):
        return (ahead_ref, back_ref)[way].at[pl.ds(r * part, part), cols]

    def direct(r, way):
        cols, to = ((high, ahead), (low, back))[way]
        j = (1, 3)[way]
        return remote(ysb.at[r, j, :, cols], landing(r, way, cols), yd_s.at[r, way], yd_r.at[r, way], to)

    def summed(r, way):
        cols, to = ((low, ahead), (high, back))[way]
        j = (1, 3)[way]
        return remote(ysb.at[r, j, :, cols], landing(r, way, cols), ys_s.at[r, way], ys_r.at[r, way], to)

    def join(r):
        for way in range(2):
            relay(r, way).wait_recv()
            j = (1, 3)[way]
            at = slice(way * hw, (way + 1) * hw)
            ysb[r, j, :, at] = (ysb[r, j, :, at].astype(F32) + rlb[r, way].astype(F32)).astype(BF)
            summed(r, way).start()

    def write(r):
        return pltpu.make_async_copy(ysb.at[r, 0], own_ref.at[pl.ds(r * part, part), :], out_s.at[r])

    for r in range(NR):
        send_att(r).wait_recv()
        for j in ORDER:
            value = half_sum[j, r * part:(r + 1) * part, :] + dot(attp[r], w2[j, width:, :])
            ysb[r, j] = value.astype(BF)
            if j == 2:
                relay(r, 0).start()
                relay(r, 1).start()
            elif j:
                direct(r, j // 2).start()
            else:
                write(r).start()
        if r:
            join(r - 1)
    join(NR - 1)
    for r in range(NR):
        for way in range(2):
            direct(r, way).wait_recv()
            summed(r, way).wait_recv()

    for r in range(NR):
        write(r).wait()
        send_att(r).wait_send()
        for way in range(2):
            relay(r, way).wait_send()
            direct(r, way).wait_send()
            summed(r, way).wait_send()
    for j in range(ny):
        send_weights(j).wait_send()
        pass_weights(j).wait_send()

    def sent(k, carry):
        for i in (1, 0):
            @pl.when((zz < nz - 1) & (k < up_steps))
            def _():
                send_up(own, i, k).wait_send()

            @pl.when((k > 0) | (core == 0))
            def _():
                send_peer(own, i, k).wait_send()
        return carry
    lax.fori_loop(0, zz + 1, sent, 0)

    if wrap:
        for i in (1, 0):
            @pl.when(source)
            def _():
                first_leg(i, 0).wait_send()

            @pl.when(c == relay_at)
            def _():
                for column in range(2):
                    second_leg(i, column).wait_send()

    @pl.when(c < nhalf)
    def _():
        send_xp().wait_send()

    @pl.when(c == extra)
    def _():
        hand_over().wait_send()

    @pl.when(c == dist)
    def _():
        def body(d, carry):
            hand_out(d).wait_send()
            return carry
        lax.fori_loop(0, nhalf - 1, body, 0)


def shards(nc, nh, queries, keys_values, offsets, w_out):
    rows = queries.shape[0]
    width = QH * HD
    nhalf = nc // 2
    nz = nhalf // 2
    ny = nh // 2
    part = rows // NR
    dma = pltpu.SemaphoreType.DMA
    parts = pl.pallas_call(
        functools.partial(kernel, nc, nh, rows),
        out_shape=[jax.ShapeDtypeStruct((rows, width), BF)] * 3,
        in_specs=[pl.BlockSpec(memory_space=pl.ANY)] * 4,
        out_specs=[pl.BlockSpec(memory_space=pl.ANY)] * 3,
        scratch_shapes=[
            pltpu.VMEM(queries.shape, BF),
            pltpu.VMEM((rows, HD), BF),
            pltpu.SMEM(offsets.shape, jnp.int32),
            dma((4,)),
            pltpu.VMEM((QH * rows, HD), BF),
            pltpu.VMEM((nhalf, 2, rows, HD), BF),
            pltpu.VMEM((rows, HD), jnp.int32),
            pltpu.VMEM((QH * rows, HD), F32),
            pltpu.VMEM((QH * rows, 2 * HD), F32),
            pltpu.VMEM((ny, 2 * width, width), BF),
            pltpu.VMEM((NR, part, width), BF),
            pltpu.VMEM((NR, part, width), BF),
            pltpu.VMEM((ny, rows, width), F32),
            pltpu.VMEM((NR, ny, part, width), BF),
            pltpu.VMEM((NR, 2, part, width // 2), BF),
            pltpu.VMEM((2, 2, rows, HD), BF),
            pltpu.VMEM((16, HD), BF),
            pltpu.VMEM((2 * QH, HD), F32),
            pltpu.VMEM((nhalf, 2 * QH, HD), F32),
            dma((nz, 2)), dma((nz, 2)), dma((nhalf, 2)),
            dma((ny,)), dma((ny,)), dma((ny,)), dma((ny,)), dma((ny,)),
            dma((NR,)), dma((NR,)),
            dma((NR, 2)), dma((NR, 2)), dma((NR, 2)),
            dma((NR, 2)), dma((NR, 2)), dma((NR, 2)),
            dma((NR,)), pltpu.SemaphoreType.REGULAR,
            dma((2,)), dma((2, 2)), dma((2, 2)),
            dma((nhalf,)), dma, dma, dma((nhalf,)),
        ],
        compiler_params=pltpu.CompilerParams(
            collective_id=0, has_side_effects=True, vmem_limit_bytes=60 * 1024 * 1024),
        cost_estimate=pl.CostEstimate(flops=4 * 10 ** 9, bytes_accessed=6 * 2 ** 20, transcendentals=4 * 2 ** 20),
    )(queries, keys_values, offsets, w_out)
    return (parts[0].astype(F32) + parts[1].astype(F32) + parts[2].astype(F32)).astype(BF)


def solution(mesh):
    nc, nh = mesh.shape["ctx"], mesh.shape["head"]

    def program(queries, keys_values, positions, offsets, w_out):
        return shards(nc, nh, queries, keys_values, offsets, w_out)

    in_specs = (
        P(("dp", "ctx"), "head"),
        P(None, ("dp", "ctx"), "head"),
        P(("dp", "ctx")),
        P("dp"),
        P("head", None),
    )
    out_specs = P(("dp", "ctx"), "head")
    return jax.shard_map(program, mesh=mesh, in_specs=in_specs, out_specs=out_specs, check_vma=False)
```

```python
import functools
import math

import jax
import jax.numpy as jnp
from jax import lax
from jax.experimental import pallas as pl
from jax.experimental.pallas import tpu as pltpu
from jax.sharding import PartitionSpec as P

HD = 128
QH = 4
NR = 2
ORDER = (2, 1, 3, 0)
ROPE_BASE = 500000.0
STRETCH = 16.0
ANCHOR_LENGTH = 8192.0
BETA_FAST = 32.0
BETA_SLOW = 1.0
MAGNITUDE = 0.1 * math.log(16.0) + 1.0
NEGATIVE = -1e30
LOG2E = 1.4426950408889634
MESH = pl.DeviceIdType.MESH
BF = jnp.bfloat16
F32 = jnp.float32


def remote(src, dst, send_sem, recv_sem, device):
    return pltpu.make_async_remote_copy(
        src_ref=src, dst_ref=dst, send_sem=send_sem, recv_sem=recv_sem,
        device_id=device, device_id_type=MESH,
    )


def dot(a, b):
    return jnp.dot(a, b, preferred_element_type=F32)


def dot_t(a, b):
    return lax.dot_general(a, b, (((1,), (1,)), ((), ())), preferred_element_type=F32)


def kernel(
    nc, nh, rows,
    q_hbm, kv_hbm, off_hbm, w_ref, own_ref, ahead_ref, back_ref,
    q_ref, k_ref, off_ref, in_s,
    qs, kvb, st, mx, acc, w2, att, attp, half_sum, ysb, rlb, pas, xq, xp, xr,
    up_s, peer_s, kv_r, wl_s, ws_s, wr_s, wf_s, wf_r, ax_s, ax_r, rl_s, rl_r, yd_s, yd_r, ys_s, ys_r, out_s, go, f1_s, f1_r, f2_s, xq_s, xq_r, xr_s, xr_r,
):
    nhalf = nc // 2
    nz = nhalf // 2
    ny = nh // 2
    part = rows // NR
    mrows = QH * part
    width = QH * HD
    wrows = width // 2
    hw = width // 2

    c = lax.axis_index("ctx")
    hd = lax.axis_index("head")
    dp = lax.axis_index("dp")
    z = c // 2
    core = c % 2
    half = z // nz
    zz = z % nz
    own = 2 * zz + core
    other = 2 * zz + 1 - core
    y = hd // 2
    x = hd % 2
    up = {"ctx": jnp.minimum(c + 2, nc - 1)}
    down = {"ctx": jnp.maximum(c - 2, 0)}
    peer = {"ctx": c + 1 - 2 * core}
    across = {"head": hd + 1 - 2 * x}
    same_dp = x == core
    w_to = {"head": hd + 1 - 2 * x, "dp": jnp.where(same_dp, dp, 1 - dp)}
    w_from = {"head": hd + 1 - 2 * x, "dp": jnp.where(same_dp, 1 - dp, dp)}
    extra = nhalf
    dist = nhalf - 1
    token = jnp.where(c == extra, 1, 0) + jnp.where(c == dist, nhalf - 1, 0)

    def along_y(j):
        return {"head": ((y + j) % ny) * 2 + x}

    barrier = pltpu.get_barrier_semaphore()

    wrap = nz == 8
    up_steps = jnp.where(half == 1, nz - 2, nz - 1) if wrap else nz - 1
    relay_at = 2 * (nz - 2)
    source = (half == 1) & (zz == 0)
    sink = (half == 1) & (zz == nz - 1)
    far = jnp.where(source, 1, 0)

    def greet(device):
        pl.semaphore_signal(barrier, inc=1, device_id=device, device_id_type=MESH)

    greet(peer)
    greet(across)
    greet(w_to)
    greet(w_from)
    for j in range(1, ny):
        greet(along_y(j))

    @pl.when(zz < nz - 1)
    def _():
        greet(up)

    @pl.when(zz > 0)
    def _():
        greet(down)

    @pl.when(c < dist)
    def _():
        greet({"ctx": jnp.int32(dist)})

    @pl.when(c == dist)
    def _():
        greet({"ctx": jnp.int32(extra)})

    if wrap:
        @pl.when(c == relay_at)
        def _():
            for column in range(2):
                greet({"ctx": jnp.int32(nhalf + column)})

        @pl.when(sink)
        def _():
            greet({"ctx": jnp.int32(relay_at)})

    order = [j for j in ORDER if j < ny]

    def own_weights(j):
        col = pl.multiple_of((((y + j) % ny) * 2 + x) * width, 128)
        return pltpu.make_async_copy(
            w_ref.at[:, pl.ds(col, width)], w2.at[j, pl.ds(0, width), :], wl_s.at[j])

    offsets_in = pltpu.make_async_copy(off_hbm, off_ref, in_s.at[0])
    keys_in = pltpu.make_async_copy(kv_hbm.at[0], k_ref, in_s.at[1])
    values_in = pltpu.make_async_copy(kv_hbm.at[1], kvb.at[own, 1], in_s.at[3])
    queries_in = pltpu.make_async_copy(q_hbm, q_ref, in_s.at[2])
    values_in.start()
    offsets_in.start()
    keys_in.start()
    queries_in.start()
    for j in range(ny):
        own_weights(j).start()

    near = 4 + (ny - 1) + token + jnp.where(zz < nz - 1, 1, 0) + jnp.where(zz > 0, 1, 0)
    if wrap:
        @pl.when(c != relay_at)
        def _():
            pl.semaphore_wait(barrier, near + far)

        @pl.when(c == relay_at + 1)
        def _():
            pl.semaphore_signal(go, inc=1, device_id=peer, device_id_type=MESH)

        @pl.when(c == relay_at + 2)
        def _():
            pl.semaphore_signal(go, inc=1, device_id=down, device_id_type=MESH)

        @pl.when(c == relay_at)
        def _():
            pl.semaphore_wait(go, 2)
    else:
        pl.semaphore_wait(barrier, near)

    def send_up(slot, i, step):
        return remote(kvb.at[slot, i], kvb.at[slot, i], up_s.at[step, i], kv_r.at[slot, i], up)

    def send_peer(slot, i, step):
        return remote(kvb.at[slot, i], kvb.at[slot, i], peer_s.at[step, i], kv_r.at[slot, i], peer)

    def send_own(i):
        @pl.when(zz < nz - 1)
        def _():
            send_up(own, i, 0).start()

        if wrap:
            for column in range(2):
                @pl.when(source & (core == column))
                def _():
                    first_leg(i, column).start()

        @pl.when(core == 0)
        def _():
            send_peer(own, i, 0).start()

    def first_leg(i, column):
        return remote(kvb.at[own, i], pas.at[column, i], f1_s.at[i], f1_r.at[column, i], {"ctx": jnp.int32(relay_at)})

    def second_leg(i, column):
        return remote(
            pas.at[column, i], kvb.at[column, i], f2_s.at[column, i], kv_r.at[column, i],
            {"ctx": jnp.int32(nhalf + 2 * (nz - 1) + column)})

    values_in.wait()
    send_own(1)

    lane = lax.broadcasted_iota(jnp.int32, (rows, HD), 1)
    token = lax.broadcasted_iota(jnp.int32, (rows, HD), 0) + c * rows
    start = jnp.zeros((rows, HD), jnp.int32)
    offsets_in.wait()
    for d in range(off_ref.shape[0]):
        o = off_ref[d]
        start = jnp.maximum(start, jnp.where(token >= o, o, 0))
    st[...] = start
    index = (lax.broadcasted_iota(jnp.int32, (8, HD), 1) % (HD // 2)).astype(F32)
    base = jnp.exp(index * (-2.0 * math.log(ROPE_BASE) / HD))
    ramp = jnp.clip((base * (ANCHOR_LENGTH / (2.0 * math.pi)) - BETA_SLOW) / (BETA_FAST - BETA_SLOW), 0.0, 1.0)
    freq = base * (1.0 - ramp) / STRETCH + base * ramp
    angle = (token - start).astype(F32) * freq[0:1]
    cosine = jnp.cos(angle) * MAGNITUDE
    sine = jnp.sin(angle) * jnp.where(lane < HD // 2, -MAGNITUDE, MAGNITUDE)

    def rotate(field):
        field = field.astype(F32)
        return field * cosine + pltpu.roll(field, HD // 2, 1) * sine

    keys_in.wait()
    kvb[own, 0] = rotate(k_ref[...]).astype(BF)
    send_own(0)

    if wrap:
        @pl.when(c == relay_at)
        def _():
            pl.semaphore_wait(barrier, near + 2)

    wrow = pl.multiple_of(core * wrows, 128)
    wback = pl.multiple_of((1 - core) * wrows, 128)

    def send_weights(j):
        col = pl.multiple_of((((y + j) % ny) * 2 + 1 - x) * width, 128)
        return remote(
            w_ref.at[pl.ds(wrow, wrows), pl.ds(col, width)],
            w2.at[j, pl.ds(width + wrow, wrows), :], ws_s.at[j], wr_s.at[j], w_to)

    def pass_weights(j):
        at = w2.at[j, pl.ds(width + wrow, wrows), :]
        return remote(at, at, wf_s.at[j], wf_r.at[j], peer)

    def passed_weights(j):
        at = w2.at[j, pl.ds(width + wback, wrows), :]
        return remote(at, at, wf_s.at[j], wf_r.at[j], peer)

    for j in order:
        send_weights(j).start()

    def forward_weights(j):
        send_weights(j).wait_recv()
        pass_weights(j).start()

    scale = HD ** (-0.5) * LOG2E
    queries_in.wait()
    for h in range(QH):
        rot = (rotate(q_ref[:, h * HD:(h + 1) * HD]) * scale).astype(BF)
        for r in range(NR):
            at = r * mrows + h * part
            qs[at:at + part, :] = rot[r * part:(r + 1) * part]

    def hand_over():
        return remote(xq, xq, xq_s.at[0], xq_r, {"ctx": jnp.int32(dist)})

    def hand_out(d):
        return remote(xq, xq, xq_s.at[d], xq_r, {"ctx": d})

    @pl.when(c == extra)
    def _():
        heads = [qs[h * part:h * part + 1, :] for h in range(QH)]
        xq[...] = jnp.concatenate(heads + [jnp.zeros((16 - QH, HD), BF)], axis=0)
        hand_over().start()

    @pl.when(c == dist)
    def _():
        hand_out(0).wait_recv()

        def body(d, carry):
            hand_out(d).start()
            return carry
        lax.fori_loop(0, nhalf - 1, body, 0)

    def with_ones(v):
        return jnp.concatenate([v, jnp.ones(v.shape, BF)], axis=1)

    def wide(v, n):
        return jnp.tile(v, (1, n))

    def starts_of(t):
        return jnp.concatenate([st[t * part:(t + 1) * part, :]] * QH, axis=0)

    def tokens_of(t, n):
        i = lax.broadcasted_iota(jnp.int32, (mrows, n), 0) % part
        return i + (c * rows + t * part)

    for t in range(NR):
        at = slice(t * mrows, (t + 1) * mrows)
        s = dot_t(qs[at, :], kvb[own, 0])
        key = lax.broadcasted_iota(jnp.int32, (mrows, rows), 1) + c * rows
        seen = (key <= tokens_of(t, rows)) & (key >= wide(starts_of(t), rows // HD))
        s = jnp.where(seen, s, NEGATIVE)
        m = jnp.broadcast_to(jnp.max(s, axis=1, keepdims=True), (mrows, HD))
        p = jnp.exp2(s - wide(m, rows // HD)).astype(BF)
        mx[at, :] = m
        acc[at, :] = dot(p, with_ones(kvb[own, 1]))

    def update(first, keys, values, masked, tiles=range(NR)):
        n = keys.shape[0]
        values = with_ones(values)
        for t in tiles:
            at = slice(t * mrows, (t + 1) * mrows)
            s = dot_t(qs[at, :], keys)
            if masked:
                key = lax.broadcasted_iota(jnp.int32, (mrows, n), 1) + first
                s = jnp.where(key >= wide(starts_of(t), n // HD), s, NEGATIVE)
            before = mx[at, :]
            m = jnp.maximum(before, jnp.max(s, axis=1, keepdims=True))
            p = jnp.exp2(s - wide(m, n // HD)).astype(BF)
            alpha = jnp.exp2(before - m)
            mx[at, :] = m
            acc[at, :] = acc[at, :] * wide(alpha, 2) + dot(p, values)

    def send_xp():
        return remote(xp, xr.at[own], xr_s, xr_r.at[own], {"ctx": jnp.int32(extra)})

    def answer_token():
        @pl.when(c != dist)
        def _():
            hand_over().wait_recv()

        s = dot_t(xq[...], kvb[own, 0])
        m = jnp.broadcast_to(jnp.max(s, axis=1, keepdims=True), (16, HD))
        p = jnp.exp2(s - wide(m, rows // HD)).astype(BF)
        sums = dot(p, with_ones(kvb[own, 1]))
        xp[0:QH, :] = sums[0:QH, 0:HD]
        xp[QH:2 * QH, :] = jnp.where(lane[0:QH] < HD // 2, m[0:QH], sums[0:QH, HD:])
        send_xp().start()

    @pl.when(core == 1)
    def _():
        for i in (1, 0):
            send_peer(other, i, 0).wait_recv()
        update((c - 1) * rows, kvb[other, 0], kvb[other, 1], True)

    steps = jnp.minimum(zz, up_steps)

    def both(chip):
        for i in (1, 0):
            send_peer(2 * chip + 1 - core, i, 0).wait_recv()
        keys = jnp.concatenate([kvb[2 * chip, 0], kvb[2 * chip + 1, 0]], axis=0)
        values = jnp.concatenate([kvb[2 * chip, 1], kvb[2 * chip + 1, 1]], axis=0)

        @pl.when(half == 0)
        def _():
            update(0, keys, values, False)

        @pl.when(half == 1)
        def _():
            update((half * nhalf + 2 * chip) * rows, keys, values, True)

    def step(k, carry):
        mine = 2 * (zz - k) + core
        for i in (1, 0):
            send_up(mine, i, 0).wait_recv()

            @pl.when((zz < nz - 1) & (k < up_steps))
            def _():
                send_up(mine, i, k).start()
            send_peer(mine, i, k).start()

        @pl.when(k > 1)
        def _():
            both(zz - k + 1)

        @pl.when((k == 3) & (zz > 3) & (c < nhalf))
        def _():
            answer_token()

        for i, j in enumerate(order):
            @pl.when(k == i + 2)
            def _():
                forward_weights(j)

        if wrap:
            @pl.when(sink & (k == nz - 3))
            def _():
                for i in (1, 0):
                    send_peer(core, i, 0).wait_recv()
                    send_peer(core, i, nz - 1).start()

            @pl.when(sink & (k == nz - 2))
            def _():
                both(0)

            @pl.when((c == relay_at) & (k == 2))
            def _():
                for column in range(2):
                    for i in (1, 0):
                        first_leg(i, column).wait_recv()
                        second_leg(i, column).start()
        return carry

    lax.fori_loop(1, steps + 1, step, 0)

    @pl.when((zz <= 3) & (c < nhalf))
    def _():
        answer_token()

    for i, j in enumerate(order):
        @pl.when(steps < i + 2)
        def _():
            forward_weights(j)

    @pl.when(c == extra)
    def _():
        def arrived(d, carry):
            remote(xp, xr.at[d], xr_s, xr_r.at[d], {"ctx": jnp.int32(0)}).wait_recv()
            return carry
        lax.fori_loop(0, nhalf, arrived, 0)
        mo = jnp.concatenate([mx[h * part:h * part + 1, :] for h in range(QH)], axis=0)
        ao = jnp.concatenate([acc[h * part:h * part + 1, :] for h in range(QH)], axis=0)
        tops = [jnp.broadcast_to(xr[d, QH:2 * QH, 0:1], (QH, HD)) for d in range(nhalf)]
        m = functools.reduce(jnp.maximum, tops, mo)
        total = ao * wide(jnp.exp2(mo - m), 2)
        for d in range(nhalf):
            weight = jnp.broadcast_to(xr[d, QH:2 * QH, HD // 2:HD // 2 + 1], (QH, HD))
            total = total + jnp.concatenate([xr[d, 0:QH, :], weight], axis=1) * wide(jnp.exp2(tops[d] - m), 2)
        for h in range(QH):
            acc[h * part:h * part + 1, :] = total[h:h + 1, :]

    def send_att(r):
        return remote(att.at[r], attp.at[r], ax_s.at[r], ax_r.at[r], across)

    def last(slot, tiles):
        @pl.when((zz > 0) & (half == 0))
        def _():
            update(0, kvb[slot, 0], kvb[slot, 1], False, tiles)

        @pl.when((zz > 0) & (half == 1))
        def _():
            update((half * nhalf + slot) * rows, kvb[slot, 0], kvb[slot, 1], True, tiles)

    bottom = 2 * (zz - steps)
    last(bottom + core, range(NR))

    @pl.when(zz > 0)
    def _():
        for i in (1, 0):
            send_peer(bottom + 1 - core, i, 0).wait_recv()

    for r in range(NR):
        last(bottom + 1 - core, [r])
        for h in range(QH):
            at = r * mrows + h * part
            block = acc[at:at + part, :]
            att[r, :, h * HD:(h + 1) * HD] = (block[:, 0:HD] / block[:, HD:]).astype(BF)
        send_att(r).start()

    for j in order:
        own_weights(j).wait()
        half_sum[j] = dot(att[...].reshape(rows, width), w2[j, 0:width, :])
    for j in order:
        passed_weights(j).wait_recv()

    low, high = pl.ds(0, hw), pl.ds(hw, hw)
    ahead, back = along_y(1), along_y(ny - 1)

    def relay(r, way):
        cols, to = ((low, ahead), (high, back))[way]
        return remote(ysb.at[r, 2, :, cols], rlb.at[r, way], rl_s.at[r, way], rl_r.at[r, way], to)

    def landing(r, way, cols):
        return (ahead_ref, back_ref)[way].at[pl.ds(r * part, part), cols]

    def direct(r, way):
        cols, to = ((high, ahead), (low, back))[way]
        j = (1, 3)[way]
        return remote(ysb.at[r, j, :, cols], landing(r, way, cols), yd_s.at[r, way], yd_r.at[r, way], to)

    def summed(r, way):
        cols, to = ((low, ahead), (high, back))[way]
        j = (1, 3)[way]
        return remote(ysb.at[r, j, :, cols], landing(r, way, cols), ys_s.at[r, way], ys_r.at[r, way], to)

    def join(r):
        for way in range(2):
            relay(r, way).wait_recv()
            j = (1, 3)[way]
            at = slice(way * hw, (way + 1) * hw)
            ysb[r, j, :, at] = (ysb[r, j, :, at].astype(F32) + rlb[r, way].astype(F32)).astype(BF)
            summed(r, way).start()

    def write(r):
        return pltpu.make_async_copy(ysb.at[r, 0], own_ref.at[pl.ds(r * part, part), :], out_s.at[r])

    for r in range(NR):
        send_att(r).wait_recv()
        for j in ORDER:
            value = half_sum[j, r * part:(r + 1) * part, :] + dot(attp[r], w2[j, width:, :])
            ysb[r, j] = value.astype(BF)
            if j == 2:
                relay(r, 0).start()
                relay(r, 1).start()
            elif j:
                direct(r, j // 2).start()
            else:
                write(r).start()
        if r:
            join(r - 1)
    join(NR - 1)
    for r in range(NR):
        for way in range(2):
            direct(r, way).wait_recv()
            summed(r, way).wait_recv()

    for r in range(NR):
        write(r).wait()
        send_att(r).wait_send()
        for way in range(2):
            relay(r, way).wait_send()
            direct(r, way).wait_send()
            summed(r, way).wait_send()
    for j in range(ny):
        send_weights(j).wait_send()
        pass_weights(j).wait_send()

    def sent(k, carry):
        for i in (1, 0):
            @pl.when((zz < nz - 1) & (k < up_steps))
            def _():
                send_up(own, i, k).wait_send()

            @pl.when((k > 0) | (core == 0))
            def _():
                send_peer(own, i, k).wait_send()
        return carry
    lax.fori_loop(0, zz + 1, sent, 0)

    if wrap:
        for i in (1, 0):
            @pl.when(source)
            def _():
                first_leg(i, 0).wait_send()

            @pl.when(c == relay_at)
            def _():
                for column in range(2):
                    second_leg(i, column).wait_send()

    @pl.when(c < nhalf)
    def _():
        send_xp().wait_send()

    @pl.when(c == extra)
    def _():
        hand_over().wait_send()

    @pl.when(c == dist)
    def _():
        def body(d, carry):
            hand_out(d).wait_send()
            return carry
        lax.fori_loop(0, nhalf - 1, body, 0)


def shards(nc, nh, queries, keys_values, offsets, w_out):
    rows = queries.shape[0]
    width = QH * HD
    nhalf = nc // 2
    nz = nhalf // 2
    ny = nh // 2
    part = rows // NR
    dma = pltpu.SemaphoreType.DMA
    parts = pl.pallas_call(
        functools.partial(kernel, nc, nh, rows),
        out_shape=[jax.ShapeDtypeStruct((rows, width), BF)] * 3,
        in_specs=[pl.BlockSpec(memory_space=pl.ANY)] * 4,
        out_specs=[pl.BlockSpec(memory_space=pl.ANY)] * 3,
        scratch_shapes=[
            pltpu.VMEM(queries.shape, BF),
            pltpu.VMEM((rows, HD), BF),
            pltpu.SMEM(offsets.shape, jnp.int32),
            dma((4,)),
            pltpu.VMEM((QH * rows, HD), BF),
            pltpu.VMEM((nhalf, 2, rows, HD), BF),
            pltpu.VMEM((rows, HD), jnp.int32),
            pltpu.VMEM((QH * rows, HD), F32),
            pltpu.VMEM((QH * rows, 2 * HD), F32),
            pltpu.VMEM((ny, 2 * width, width), BF),
            pltpu.VMEM((NR, part, width), BF),
            pltpu.VMEM((NR, part, width), BF),
            pltpu.VMEM((ny, rows, width), F32),
            pltpu.VMEM((NR, ny, part, width), BF),
            pltpu.VMEM((NR, 2, part, width // 2), BF),
            pltpu.VMEM((2, 2, rows, HD), BF),
            pltpu.VMEM((16, HD), BF),
            pltpu.VMEM((2 * QH, HD), F32),
            pltpu.VMEM((nhalf, 2 * QH, HD), F32),
            dma((nz, 2)), dma((nz, 2)), dma((nhalf, 2)),
            dma((ny,)), dma((ny,)), dma((ny,)), dma((ny,)), dma((ny,)),
            dma((NR,)), dma((NR,)),
            dma((NR, 2)), dma((NR, 2)), dma((NR, 2)),
            dma((NR, 2)), dma((NR, 2)), dma((NR, 2)),
            dma((NR,)), pltpu.SemaphoreType.REGULAR,
            dma((2,)), dma((2, 2)), dma((2, 2)),
            dma((nhalf,)), dma, dma, dma((nhalf,)),
        ],
        compiler_params=pltpu.CompilerParams(
            collective_id=0, has_side_effects=True, vmem_limit_bytes=60 * 1024 * 1024),
        cost_estimate=pl.CostEstimate(flops=4 * 10 ** 9, bytes_accessed=6 * 2 ** 20, transcendentals=4 * 2 ** 20),
    )(queries, keys_values, offsets, w_out)
    return (parts[0].astype(F32) + parts[1].astype(F32) + parts[2].astype(F32)).astype(BF)


def solution(mesh):
    nc, nh = mesh.shape["ctx"], mesh.shape["head"]

    def program(queries, keys_values, positions, offsets, w_out):
        return shards(nc, nh, queries, keys_values, offsets, w_out)

    in_specs = (
        P(("dp", "ctx"), "head"),
        P(None, ("dp", "ctx"), "head"),
        P(("dp", "ctx")),
        P("dp"),
        P("head", None),
    )
    out_specs = P(("dp", "ctx"), "head")
    return jax.shard_map(program, mesh=mesh, in_specs=in_specs, out_specs=out_specs, check_vma=False)
```
